32 devices in a mesh: member: 2 (over x), gx: 16 (over z, y, core).
Axes of the slice: x: 2, y: 2, z: 4, core: 2. Of those that a mesh axis runs over, the one named last changes fastest.
Arguments:
- right_side: float32 [32, 32, 64, 128], P(('member', 'gx')), parts along dimension 0, may hold values from -120 to 120
- cell_kind: int32 [32, 32, 64, 128], P(('member', 'gx')), parts along dimension 0, may hold values from 0 to 4
Outputs:
- solution_field: float32 [32, 32, 64, 128], P(('member', 'gx')), parts along dimension 0
- residual: float32 [32, 32, 64, 128], P(('member', 'gx')), parts along dimension 0
- residual_norms: float32 [4], P('member'), parts along dimension 0
The draws below stay inside these ranges and needn't reach their ends.
There are 2 independent parts, one for each index of `member`. The reference program is written for one: setup_inputs(seed, part) draws one part's arguments, and reference() takes and returns one part's arrays. A program takes and returns all parts, laid end to end along the dimension named above; each array names one. Nothing has to cross between parts.
All inputs are finite; a program needn't handle non-finite values.
Results may differ from the reference program's by a relative error of at most 0.013.
Values sent between devices are 32-bit elements; how exact they have to be, the bound alone decides.
A program may use at most 64 MiB of HBM per device.

```python
import jax
import jax.numpy as jnp

GYB = 8
BX = 32
BY = 64
NZ = 128
ITERS = 2
NX = 64
NY = 512
N_GX = 16


def grid_to_blocks(grid):
    block_rows = grid.shape[0] // BX
    return grid.reshape(block_rows, BX, GYB, BY, NZ).transpose(0, 2, 1, 3, 4).reshape(block_rows * GYB, BX, BY, NZ)


def draw_right_side(key, part):
    key = jax.random.fold_in(key, 7)
    first_key, second_key = jax.random.split(key, 2)
    xpos = jnp.arange(NX, dtype=jnp.float32) / NX
    along = jnp.exp(jnp.log(10.0) * xpos)[:, None, None]
    across = jnp.exp(jax.random.uniform(second_key, (NY,), minval=0.0, maxval=jnp.log(3.0)))[None, :, None]
    base = jnp.clip(jax.random.normal(first_key, (NX, NY, NZ)), -4.0, 4.0)
    return grid_to_blocks((base * along * across).astype(jnp.float32))


def touch_ends(array, own_key, least, high):
    index_at = [jax.random.randint(jax.random.fold_in(own_key, axis), (), 0, length) for axis, length in enumerate(array.shape)]
    widest = array.shape.index(max(array.shape))
    next_to = index_at[:widest] + [(index_at[widest] + 1) % array.shape[widest]] + index_at[widest + 1:]
    return array.at[tuple(index_at)].set(least).at[tuple(next_to)].set(high)


def setup_inputs(seed: int = 0, part: int = 0) -> dict:
    arg_keys = jax.random.split(jax.random.key(seed), 3)
    part_splits = jax.random.split(jax.random.fold_in(arg_keys[2], part), 3)
    return {
        "right_side": draw_right_side(jax.random.fold_in(jax.random.fold_in(arg_keys[2], part), 71), part),
        "cell_kind": touch_ends(jax.random.randint(part_splits[1], (N_GX, BX, BY, NZ), 0, 5), jax.random.fold_in(part_splits[1], 1), 0, 4).astype(jnp.int32),
    }


CLASS_VALUES = (0.0, 0.5, 1.0, 2.0, 4.0)
SHIFT_TERM = 0.1


def to_grid(blocks):
    block_rows = blocks.shape[0] // GYB
    return blocks.reshape(block_rows, GYB, BX, BY, NZ).transpose(0, 2, 1, 3, 4).reshape(block_rows * BX, GYB * BY, NZ)


def to_blocks(grid):
    block_rows = grid.shape[0] // BX
    return grid.reshape(block_rows, BX, GYB, BY, NZ).transpose(0, 2, 1, 3, 4).reshape(block_rows * GYB, BX, BY, NZ)


def conductivity_of(cell_kind):
    result = jnp.zeros(cell_kind.shape, jnp.float32)
    for number, value in enumerate(CLASS_VALUES):
        result = result + jnp.where(cell_kind == number, value, 0.0).astype(jnp.float32)
    return result


def harmonic(first, second):
    return 2.0 * first * second / jnp.maximum(first + second, 0.5)


def face_fields(conductivity, padded):
    return (harmonic(conductivity, padded[2:, 1:-1, 1:-1]), harmonic(conductivity, padded[:-2, 1:-1, 1:-1]),
            harmonic(conductivity, padded[1:-1, 2:, 1:-1]), harmonic(conductivity, padded[1:-1, :-2, 1:-1]),
            harmonic(conductivity, padded[1:-1, 1:-1, 2:]), harmonic(conductivity, padded[1:-1, 1:-1, :-2]))


def neighbour_sum(face_list, padded):
    total = face_list[0] * padded[2:, 1:-1, 1:-1] + face_list[1] * padded[:-2, 1:-1, 1:-1]
    total = total + face_list[2] * padded[1:-1, 2:, 1:-1] + face_list[3] * padded[1:-1, :-2, 1:-1]
    total = total + face_list[4] * padded[1:-1, 1:-1, 2:] + face_list[5] * padded[1:-1, 1:-1, :-2]
    return total


def operate_field(field, face_list, fluid_mask, diagonal_sum):
    padded = jnp.pad(field, 1)
    return jnp.where(fluid_mask, diagonal_sum * field - neighbour_sum(face_list, padded), field)


def reference(right_side, cell_kind):
    right_grid = to_grid(right_side)
    kind_grid = to_grid(cell_kind)
    conductivity = conductivity_of(kind_grid)
    face_list = face_fields(conductivity, jnp.pad(conductivity, 1))
    fluid_mask = kind_grid > 0
    face_total = face_list[0] + face_list[1] + face_list[2] + face_list[3] + face_list[4] + face_list[5]
    diagonal_sum = jnp.where(fluid_mask, SHIFT_TERM + face_total, 1.0).astype(jnp.float32)
    cell_count = right_grid.shape[0] * right_grid.shape[1] * right_grid.shape[2]
    residual = jnp.where(fluid_mask, right_grid, 0.0).astype(jnp.float32)
    solution_field = jnp.zeros_like(residual)
    smoothed = residual / diagonal_sum
    applied = operate_field(smoothed, face_list, fluid_mask, diagonal_sum)
    dir_z = jnp.zeros_like(residual)
    dir_q = jnp.zeros_like(residual)
    dir_s = jnp.zeros_like(residual)
    dir_p = jnp.zeros_like(residual)
    norms = []
    gamma_old = None
    alpha_old = None
    for index_step in range(ITERS):
        gamma_now = jnp.sum(residual * smoothed)
        delta_now = jnp.sum(applied * smoothed)
        res_sq = jnp.sum(residual * residual)
        norms.append(res_sq / cell_count)
        scaled = applied / diagonal_sum
        scaled_image = operate_field(scaled, face_list, fluid_mask, diagonal_sum)
        if index_step == 0:
            beta_now = jnp.zeros((), jnp.float32)
            alpha_now = gamma_now / delta_now
        else:
            beta_now = gamma_now / gamma_old
            alpha_now = gamma_now / (delta_now - beta_now * gamma_now / alpha_old)
        dir_z = scaled_image + beta_now * dir_z
        dir_q = scaled + beta_now * dir_q
        dir_s = applied + beta_now * dir_s
        dir_p = smoothed + beta_now * dir_p
        solution_field = solution_field + alpha_now * dir_p
        residual = residual - alpha_now * dir_s
        smoothed = smoothed - alpha_now * dir_q
        applied = applied - alpha_now * dir_z
        gamma_old = gamma_now
        alpha_old = alpha_now
    return to_blocks(solution_field), to_blocks(residual), jnp.stack(norms).astype(jnp.float32)
```

```python
import functools

import jax
import jax.numpy as jnp
from jax import lax
from jax.experimental import pallas as pl
from jax.experimental.pallas import tpu as pltpu
from jax.sharding import PartitionSpec as P

GYB = 8
SHIFT_TERM = 0.1
PAD = 8
MESH = pl.DeviceIdType.MESH


def inverse(value):
    guess = pl.reciprocal(value, approx=True)
    return guess * (2.0 - value * guess)


def conductivity_of(kind):
    power = jnp.left_shift(jnp.ones_like(kind), kind).astype(jnp.float32) * 0.25
    return jnp.where(kind > 0, power, 0.0)


def harmonic(first, second):
    return (2.0 * first) * second * inverse(jnp.maximum(first + second, 0.5))


def fold(value):
    return jnp.sum(value.reshape(-1, 8, value.shape[-1]), axis=0)


def kernel(
    n, kind_hbm, right_hbm, x_ref, r_ref, norm_ref,
    kind, right, cond, face_x, face_y, face_z, inv, smooth, image, scaled, second,
    kind_x, kind_y, send_kind_y, smooth_y, send_smooth_y, scaled_y, send_scaled_y,
    dots, in_sem, send_sem, recv_sem, dot_send, dot_recv,
):
    bx, by, nz = kind.shape
    rows = pl.ds(PAD, by)
    me = lax.axis_index("gx")
    column = lax.rem(me, GYB)
    line = lax.div(me, GYB)
    lines = n // GYB
    receives = (line > 0, line < lines - 1, column > 0, column < GYB - 1)
    sends = (line < lines - 1, line > 0, column < GYB - 1, column > 0)
    targets = (me + GYB, me - GYB, me + 1, me - 1)

    load_kind = pltpu.make_async_copy(kind_hbm.at[0], kind, in_sem.at[0])
    load_right = pltpu.make_async_copy(right_hbm.at[0], right, in_sem.at[1])
    load_kind.start()
    load_right.start()

    barrier = pltpu.get_barrier_semaphore()

    def greet(k, _):
        pl.semaphore_signal(
            barrier, inc=1, device_id={"gx": lax.rem(me + k, n)}, device_id_type=MESH
        )
        return 0

    lax.fori_loop(1, n, greet, 0)

    def copy(phase, side, src, dst):
        return pltpu.make_async_remote_copy(
            src_ref=src, dst_ref=dst,
            send_sem=send_sem.at[phase, side], recv_sem=recv_sem.at[phase, side],
            device_id={"gx": targets[side]}, device_id_type=MESH,
        )

    copies = (
        (
            copy(0, 0, kind_hbm.at[0, bx - 1], kind_x.at[0]),
            copy(0, 1, kind_hbm.at[0, 0], kind_x.at[1]),
            copy(0, 2, send_kind_y.at[1], kind_y.at[0]),
            copy(0, 3, send_kind_y.at[0], kind_y.at[1]),
        ),
        (
            copy(1, 0, smooth.at[bx, rows], smooth.at[0, rows]),
            copy(1, 1, smooth.at[1, rows], smooth.at[bx + 1, rows]),
            copy(1, 2, send_smooth_y.at[1], smooth_y.at[0]),
            copy(1, 3, send_smooth_y.at[0], smooth_y.at[1]),
        ),
        (
            copy(2, 0, scaled.at[bx, rows], scaled.at[0, rows]),
            copy(2, 1, scaled.at[1, rows], scaled.at[bx + 1, rows]),
            copy(2, 2, send_scaled_y.at[1], scaled_y.at[0]),
            copy(2, 3, send_scaled_y.at[0], scaled_y.at[1]),
        ),
    )

    def start(phase, sides):
        for side in sides:
            pl.when(sends[side])(copies[phase][side].start)

    def arrive(phase, sides):
        for side in sides:
            pl.when(receives[side])(copies[phase][side].wait_recv)

    for side in (0, 1):
        @pl.when(jnp.logical_not(receives[side]))
        def _():
            kind_x[side] = jnp.zeros((by, nz), jnp.int32)
            smooth[side * (bx + 1), rows] = jnp.zeros((by, nz), jnp.float32)
            scaled[side * (bx + 1), rows] = jnp.zeros((by, nz), jnp.float32)

        @pl.when(jnp.logical_not(receives[side + 2]))
        def _():
            kind_y[side] = jnp.zeros((bx, 1, nz), jnp.int32)
            smooth_y[side] = jnp.zeros((bx, 1, nz), jnp.float32)
            scaled_y[side] = jnp.zeros((bx, 1, nz), jnp.float32)

    pl.semaphore_wait(barrier, n - 1)
    load_kind.wait()

    def take_edges(i, _):
        send_kind_y[0, i] = kind[i, 0:1, :]
        send_kind_y[1, i] = kind[i, by - 1:by, :]
        return 0

    lax.fori_loop(0, bx, take_edges, 0, unroll=8)
    start(0, (2, 3, 0, 1))

    def conduct(i, _):
        cond[i + 1, rows] = conductivity_of(kind[i])
        return 0

    lax.fori_loop(0, bx, conduct, 0, unroll=2)

    last_lane = lax.broadcasted_iota(jnp.int32, (by, nz), 1) == nz - 1

    def inner_faces(i, _):
        own = cond[i + 1, rows]
        above = jnp.where(last_lane, 0.0, pltpu.roll(own, nz - 1, 1))
        face_z[i] = harmonic(own, above)

        @pl.when(i > 0)
        def _():
            face_x[i] = harmonic(own, cond[i, rows])
        return 0

    lax.fori_loop(0, bx, inner_faces, 0)

    arrive(0, (2, 3))

    def put_kind(i, _):
        cond[i + 1, PAD - 1:PAD, :] = conductivity_of(kind_y[0, i])
        cond[i + 1, PAD + by:PAD + by + 1, :] = conductivity_of(kind_y[1, i])
        return 0

    lax.fori_loop(0, bx, put_kind, 0, unroll=8)
    load_right.wait()
    arrive(0, (0, 1))
    face_x[0] = harmonic(cond[1, rows], conductivity_of(kind_x[0]))
    face_x[bx] = harmonic(cond[bx, rows], conductivity_of(kind_x[1]))

    def prepare(i, sums):
        res_sq, gamma = sums
        own = cond[i + 1, rows]
        face_y[i] = harmonic(
            cond[i + 1, PAD:2 * PAD + by, :], cond[i + 1, PAD - 1:2 * PAD + by - 1, :]
        )
        up = face_z[i]
        total = face_x[i] + face_x[i + 1]
        total = total + (face_y[i, 0:by, :] + face_y[i, 1:by + 1, :])
        total = total + (up + pltpu.roll(up, 1, 1))
        fluid = own > 0.0
        diagonal_inverse = inverse(jnp.where(fluid, SHIFT_TERM + total, 1.0))
        residual = jnp.where(fluid, right[i], 0.0)
        value = residual * diagonal_inverse
        right[i] = residual
        inv[i] = diagonal_inverse
        smooth[i + 1, rows] = value
        send_smooth_y[0, i] = value[0:1, :]
        send_smooth_y[1, i] = value[by - 1:by, :]
        return res_sq + fold(residual * residual), gamma + fold(residual * value)

    def neighbour_sum(field, i):
        own = field[i + 1, rows]
        up = face_z[i]
        total = face_x[i] * field[i, rows] + face_x[i + 1] * field[i + 2, rows]
        total = total + face_y[i, 0:by, :] * field[i + 1, PAD - 1:PAD + by - 1, :]
        total = total + face_y[i, 1:by + 1, :] * field[i + 1, PAD + 1:PAD + by + 1, :]
        total = total + up * pltpu.roll(own, nz - 1, 1) + pltpu.roll(up * own, 1, 1)
        return own, total

    def apply(i, sums):
        delta, cross, square, mu = sums
        own, total = neighbour_sum(smooth, i)
        residual = right[i]
        value = residual - total
        other = value * inv[i]
        image[i] = value
        scaled[i + 1, rows] = other
        send_scaled_y[0, i] = other[0:1, :]
        send_scaled_y[1, i] = other[by - 1:by, :]
        return (
            delta + fold(value * own), cross + fold(residual * value),
            square + fold(value * value), mu + fold(value * other),
        )

    def apply_again(i, nu):
        own, total = neighbour_sum(scaled, i)
        value = image[i] - total
        second[i] = value
        return nu + fold(value * own)

    def spread(buffer, field):
        def put(i, _):
            field[i + 1, PAD - 1:PAD, :] = buffer[0, i]
            field[i + 1, PAD + by:PAD + by + 1, :] = buffer[1, i]
            return 0

        lax.fori_loop(0, bx, put, 0, unroll=8)

    zero = jnp.zeros((8, nz), jnp.float32)
    sums = prepare(bx - 1, prepare(0, (zero, zero)))
    start(1, (0, 1))
    res_sq, gamma = lax.fori_loop(1, bx - 1, prepare, sums)
    start(1, (2, 3))
    arrive(1, (2, 3))
    spread(smooth_y, smooth)
    arrive(1, (0, 1))
    sums = apply(bx - 1, apply(0, (zero,) * 4))
    start(2, (0, 1))
    delta, cross, square, mu = lax.fori_loop(1, bx - 1, apply, sums)
    start(2, (2, 3))
    arrive(2, (2, 3))
    spread(scaled_y, scaled)
    nu = lax.fori_loop(1, bx - 1, apply_again, zero)
    arrive(2, (0, 1))
    nu = apply_again(bx - 1, apply_again(0, nu))

    parts = (res_sq, gamma, delta, cross, square, mu, nu)
    row = lax.broadcasted_iota(jnp.int32, (8, nz), 0)
    message = zero
    for place, part in enumerate(parts):
        message = jnp.where(row == place, jnp.sum(part, axis=0, keepdims=True), message)
    dots[me] = message

    def tell(k, _):
        pltpu.make_async_remote_copy(
            src_ref=dots.at[me], dst_ref=dots.at[me], send_sem=dot_send, recv_sem=dot_recv,
            device_id={"gx": lax.rem(me + k, n)}, device_id_type=MESH,
        ).start()
        return 0

    lax.fori_loop(1, n, tell, 0)
    most = dots.at[pl.ds(0, n - 1)]
    pltpu.make_async_copy(most, most, dot_recv).wait()

    total = jnp.sum(jnp.sum(dots[...], axis=0), axis=1, keepdims=True)
    res_sq, gamma, delta, cross, square, mu, nu = (total[k:k + 1, :] for k in range(7))
    alpha = gamma / delta
    gamma_next = gamma - 2.0 * alpha * delta + alpha * alpha * mu
    delta_next = delta - 2.0 * alpha * mu + alpha * alpha * nu
    res_sq_next = res_sq - 2.0 * alpha * cross + alpha * alpha * square
    beta = gamma_next / gamma
    alpha_next = gamma_next / (delta_next - beta * gamma_next / alpha)
    along = alpha + alpha_next * (1.0 + beta)
    across = alpha * alpha_next
    cells = n * bx * by * nz
    lane = lax.broadcasted_iota(jnp.int32, (1, nz), 1)
    norm_ref[...] = jnp.where(lane == 0, res_sq / cells, res_sq_next / cells)

    along = jnp.broadcast_to(along, (by, nz))
    across = jnp.broadcast_to(across, (by, nz))

    def finish(i, _):
        x_ref[0, i] = along * smooth[i + 1, rows] - across * scaled[i + 1, rows]
        r_ref[0, i] = right[i] - along * image[i] + across * second[i]
        return 0

    lax.fori_loop(0, bx, finish, 0, unroll=2)

    for phase in range(3):
        for side in range(4):
            pl.when(sends[side])(copies[phase][side].wait_send)
    pltpu.make_async_copy(most, most, dot_send).wait()


def body(right_side, cell_kind):
    n = lax.axis_size("gx")
    _, bx, by, nz = right_side.shape
    f32, i32 = jnp.float32, jnp.int32
    field = pltpu.VMEM((bx, by, nz), f32)
    padded = pltpu.VMEM((bx + 2, by + 2 * PAD, nz), f32)
    edges = pltpu.VMEM((2, bx, 1, nz), f32)
    x, r, norms = pl.pallas_call(
        functools.partial(kernel, n),
        out_shape=(
            jax.ShapeDtypeStruct(right_side.shape, f32),
            jax.ShapeDtypeStruct(right_side.shape, f32),
            jax.ShapeDtypeStruct((1, nz), f32),
        ),
        in_specs=[pl.BlockSpec(memory_space=pl.ANY)] * 2,
        out_specs=[pl.BlockSpec(memory_space=pltpu.VMEM)] * 3,
        scratch_shapes=[
            pltpu.VMEM((bx, by, nz), i32), field, padded,
            pltpu.VMEM((bx + 1, by, nz), f32), pltpu.VMEM((bx, by + PAD, nz), f32),
            field, field, padded, field, padded, field,
            pltpu.VMEM((2, by, nz), i32), pltpu.VMEM((2, bx, 1, nz), i32),
            pltpu.VMEM((2, bx, 1, nz), i32), edges, edges, edges, edges,
            pltpu.VMEM((n, 8, nz), f32),
            pltpu.SemaphoreType.DMA((2,)),
            pltpu.SemaphoreType.DMA((3, 4)),
            pltpu.SemaphoreType.DMA((3, 4)),
            pltpu.SemaphoreType.DMA,
            pltpu.SemaphoreType.DMA,
        ],
        compiler_params=pltpu.CompilerParams(
            collective_id=0, has_side_effects=True, vmem_limit_bytes=44 * 1024 * 1024
        ),
    )(cell_kind, right_side)
    return x, r, norms[0, :2]


def solution(mesh):
    spec = P(("member", "gx"), None, None, None)
    return jax.shard_map(
        body, mesh=mesh, in_specs=(spec, spec), out_specs=(spec, spec, P("member")),
        check_vma=False,
    )
```

```python
import functools

import jax
import jax.numpy as jnp
from jax import lax
from jax.experimental import pallas as pl
from jax.experimental.pallas import tpu as pltpu
from jax.sharding import PartitionSpec as P

GYB = 8
SHIFT_TERM = 0.1
PAD = 8
INNER_UNROLL = 1
STEP_UNROLL = 2
RIM_UNROLL = 2
MESH = pl.DeviceIdType.MESH


def inverse(value):
    guess = pl.reciprocal(value, approx=True)
    return guess * (2.0 - value * guess)


def conductivity_of(kind):
    power = jnp.left_shift(jnp.ones_like(kind), kind).astype(jnp.float32) * 0.25
    return jnp.where(kind > 0, power, 0.0)


def harmonic(first, second):
    return (2.0 * first) * second * inverse(jnp.maximum(first + second, 0.5))


def fold(value):
    return jnp.sum(value.reshape(-1, 8, value.shape[-1]), axis=0)


def kernel(
    n, kind_hbm, right_hbm, right, smooth, image, scaled, second, factors,
    kind, cond, face_x, face_y, face_z, inv,
    kind_x, smooth_x, scaled_x, kind_y, send_kind_y, smooth_y, send_smooth_y, scaled_y,
    send_scaled_y, dots, in_sem, send_sem, recv_sem, dot_send, dot_recv,
):
    bx, by, nz = kind.shape
    rows = pl.ds(PAD, by)
    me = lax.axis_index("gx")
    column = lax.rem(me, GYB)
    line = lax.div(me, GYB)
    lines = n // GYB
    receives = (line > 0, line < lines - 1, column > 0, column < GYB - 1)
    sends = (line < lines - 1, line > 0, column < GYB - 1, column > 0)
    targets = (me + GYB, me - GYB, me + 1, me - 1)

    barrier = pltpu.get_barrier_semaphore()

    def greet(k, _):
        pl.semaphore_signal(
            barrier, inc=1, device_id={"gx": lax.rem(me + k, n)}, device_id_type=MESH
        )
        return 0

    lax.fori_loop(1, n, greet, 0)

    load_kind = pltpu.make_async_copy(kind_hbm.at[0], kind, in_sem.at[0])
    load_right = pltpu.make_async_copy(right_hbm.at[0], right, in_sem.at[1])
    load_kind.start()
    load_right.start()

    def copy(phase, side, src, dst):
        return pltpu.make_async_remote_copy(
            src_ref=src, dst_ref=dst,
            send_sem=send_sem.at[phase, side], recv_sem=recv_sem.at[phase, side],
            device_id={"gx": targets[side]}, device_id_type=MESH,
        )

    copies = (
        (
            copy(0, 0, kind_hbm.at[0, bx - 1], kind_x.at[0]),
            copy(0, 1, kind_hbm.at[0, 0], kind_x.at[1]),
            copy(0, 2, send_kind_y.at[1], kind_y.at[0]),
            copy(0, 3, send_kind_y.at[0], kind_y.at[1]),
        ),
        (
            copy(1, 0, smooth.at[bx - 1, rows], smooth_x.at[0]),
            copy(1, 1, smooth.at[0, rows], smooth_x.at[1]),
            copy(1, 2, send_smooth_y.at[1], smooth_y.at[0]),
            copy(1, 3, send_smooth_y.at[0], smooth_y.at[1]),
        ),
        (
            copy(2, 0, scaled.at[bx - 1, rows], scaled_x.at[0]),
            copy(2, 1, scaled.at[0, rows], scaled_x.at[1]),
            copy(2, 2, send_scaled_y.at[1], scaled_y.at[0]),
            copy(2, 3, send_scaled_y.at[0], scaled_y.at[1]),
        ),
    )

    def start(phase, sides):
        for side in sides:
            pl.when(sends[side])(copies[phase][side].start)

    def arrive(phase, sides):
        for side in sides:
            pl.when(receives[side])(copies[phase][side].wait_recv)

    for side in (0, 1):
        @pl.when(jnp.logical_not(receives[side]))
        def _():
            kind_x[side] = jnp.zeros((by, nz), jnp.int32)
            smooth_x[side] = jnp.zeros((by, nz), jnp.float32)
            scaled_x[side] = jnp.zeros((by, nz), jnp.float32)

        @pl.when(jnp.logical_not(receives[side + 2]))
        def _():
            kind_y[side] = jnp.zeros((bx, 1, nz), jnp.int32)
            smooth_y[side] = jnp.zeros((bx, 1, nz), jnp.float32)
            scaled_y[side] = jnp.zeros((bx, 1, nz), jnp.float32)

    pl.semaphore_wait(barrier, n - 1)
    start(0, (0, 1))
    load_kind.wait()

    def take_edges(i, _):
        send_kind_y[0, i] = kind[i, 0:1, :]
        send_kind_y[1, i] = kind[i, by - 1:by, :]
        return 0

    lax.fori_loop(0, bx, take_edges, 0, unroll=8)
    start(0, (2, 3))

    def conduct(i, _):
        cond[i, rows] = conductivity_of(kind[i])
        return 0

    lax.fori_loop(0, bx, conduct, 0, unroll=4)

    last_lane = lax.broadcasted_iota(jnp.int32, (by, nz), 1) == nz - 1

    def face_along(i):
        own = cond[i, rows]
        above = jnp.where(last_lane, 0.0, pltpu.roll(own, nz - 1, 1))
        face_z[i] = harmonic(own, above)
        return own

    def inner_faces(i, _):
        own = face_along(i)
        face_x[i] = harmonic(own, cond[i - 1, rows])
        return 0

    face_along(0)
    lax.fori_loop(1, bx, inner_faces, 0, unroll=INNER_UNROLL)

    arrive(0, (2, 3))

    def put_kind(i, _):
        cond[i, PAD - 1:PAD, :] = conductivity_of(kind_y[0, i])
        cond[i, PAD + by:PAD + by + 1, :] = conductivity_of(kind_y[1, i])
        return 0

    lax.fori_loop(0, bx, put_kind, 0, unroll=8)
    load_right.wait()

    def prepare(i, sums):
        res_sq, gamma = sums
        own = cond[i, rows]
        face_y[i] = harmonic(
            cond[i, PAD:2 * PAD + by, :], cond[i, PAD - 1:2 * PAD + by - 1, :]
        )
        up = face_z[i]
        total = face_x[i] + face_x[i + 1]
        total = total + (face_y[i, 0:by, :] + face_y[i, 1:by + 1, :])
        total = total + (up + pltpu.roll(up, 1, 1))
        fluid = own > 0.0
        diagonal_inverse = inverse(jnp.where(fluid, SHIFT_TERM + total, 1.0))
        residual = jnp.where(fluid, right[i], 0.0)
        value = residual * diagonal_inverse
        right[i] = residual
        inv[i] = diagonal_inverse
        smooth[i, rows] = value
        send_smooth_y[0, i] = value[0:1, :]
        send_smooth_y[1, i] = value[by - 1:by, :]
        return res_sq + fold(residual * residual), gamma + fold(residual * value)

    def neighbour_sum(field, i, first, count, below, above):
        own = field[i, pl.ds(PAD + first, count)]
        here = pl.ds(first, count)
        up = face_z[i, here]
        total = face_x[i, here] * below + face_x[i + 1, here] * above
        total = total + face_y[i, here] * field[i, pl.ds(PAD + first - 1, count)]
        total = total + face_y[i, pl.ds(first + 1, count)] * field[i, pl.ds(PAD + first + 1, count)]
        total = total + up * pltpu.roll(own, nz - 1, 1) + pltpu.roll(up * own, 1, 1)
        return own, total

    def apply(i, sums, first=0, count=by, below=None, above=None):
        delta, cross, square, mu = sums
        here, inside = pl.ds(first, count), pl.ds(PAD + first, count)
        below = smooth[i - 1, inside] if below is None else below
        above = smooth[i + 1, inside] if above is None else above
        own, total = neighbour_sum(smooth, i, first, count, below, above)
        residual = right[i, here]
        value = residual - total
        other = value * inv[i, here]
        image[i, here] = value
        scaled[i, inside] = other
        if first == 0:
            send_scaled_y[0, i] = other[0:1, :]
        if first + count == by:
            send_scaled_y[1, i] = other[count - 1:count, :]
        return (
            delta + fold(value * own), cross + fold(residual * value),
            square + fold(value * value), mu + fold(value * other),
        )

    def apply_again(i, nu, first=0, count=by, below=None, above=None):
        here, inside = pl.ds(first, count), pl.ds(PAD + first, count)
        below = scaled[i - 1, inside] if below is None else below
        above = scaled[i + 1, inside] if above is None else above
        own, total = neighbour_sum(scaled, i, first, count, below, above)
        value = image[i, here] - total
        second[i, here] = value
        return nu + fold(value * own)

    def spread(buffer, field):
        def put(i, _):
            field[i, PAD - 1:PAD, :] = buffer[0, i]
            field[i, PAD + by:PAD + by + 1, :] = buffer[1, i]
            return 0

        lax.fori_loop(0, bx, put, 0, unroll=8)

    def middle(step, sums):
        return lax.fori_loop(
            1, bx - 1, lambda i, s: step(i, s, PAD, by - 2 * PAD), sums, unroll=STEP_UNROLL
        )

    def rims(step, sums):
        def both(i, s):
            return step(i, step(i, s, 0, PAD), by - PAD, PAD)

        return lax.fori_loop(1, bx - 1, both, sums, unroll=RIM_UNROLL)

    def ends(step, sums, field, halo):
        sums = step(0, sums, below=halo[0])
        return step(bx - 1, sums, above=halo[1])

    zero = jnp.zeros((8, nz), jnp.float32)
    sums = lax.fori_loop(1, bx - 1, prepare, (zero, zero), unroll=STEP_UNROLL)
    arrive(0, (0, 1))
    face_x[0] = harmonic(cond[0, rows], conductivity_of(kind_x[0]))
    face_x[bx] = harmonic(cond[bx - 1, rows], conductivity_of(kind_x[1]))
    res_sq, gamma = prepare(bx - 1, prepare(0, sums))
    start(1, (0, 1, 2, 3))
    sums = middle(apply, (zero,) * 4)
    arrive(1, (2, 3))
    spread(smooth_y, smooth)
    sums = rims(apply, sums)
    arrive(1, (0, 1))
    delta, cross, square, mu = ends(apply, sums, smooth, smooth_x)
    start(2, (0, 1, 2, 3))
    nu = middle(apply_again, zero)
    arrive(2, (2, 3))
    spread(scaled_y, scaled)
    nu = rims(apply_again, nu)
    arrive(2, (0, 1))
    nu = ends(apply_again, nu, scaled, scaled_x)

    parts = (res_sq, gamma, delta, cross, square, mu, nu)
    row = lax.broadcasted_iota(jnp.int32, (8, nz), 0)
    message = zero
    for place, part in enumerate(parts):
        message = jnp.where(row == place, jnp.sum(part, axis=0, keepdims=True), message)
    dots[me] = message

    def tell(k, _):
        pltpu.make_async_remote_copy(
            src_ref=dots.at[me], dst_ref=dots.at[me], send_sem=dot_send, recv_sem=dot_recv,
            device_id={"gx": lax.rem(me + k, n)}, device_id_type=MESH,
        ).start()
        return 0

    lax.fori_loop(1, n, tell, 0)
    most = dots.at[pl.ds(0, n - 1)]
    for phase in range(3):
        for side in range(4):
            pl.when(sends[side])(copies[phase][side].wait_send)
    pltpu.make_async_copy(most, most, dot_recv).wait()

    total = jnp.sum(jnp.sum(dots[...], axis=0), axis=1, keepdims=True)
    res_sq, gamma, delta, cross, square, mu, nu = (total[k:k + 1, :] for k in range(7))
    alpha = gamma / delta
    gamma_next = gamma - 2.0 * alpha * delta + alpha * alpha * mu
    delta_next = delta - 2.0 * alpha * mu + alpha * alpha * nu
    res_sq_next = res_sq - 2.0 * alpha * cross + alpha * alpha * square
    beta = gamma_next / gamma
    alpha_next = gamma_next / (delta_next - beta * gamma_next / alpha)
    along = alpha + alpha_next * (1.0 + beta)
    across = alpha * alpha_next
    cells = n * bx * by * nz
    result = jnp.where(row == 0, along, across)
    result = jnp.where(row == 2, res_sq / cells, result)
    factors[...] = jnp.where(row == 3, res_sq_next / cells, result)
    pltpu.make_async_copy(most, most, dot_send).wait()


def finish(right, smooth, image, scaled, second, factors, x_hbm, r_hbm, norms, x, r, sems):
    bx, by, nz = right.shape
    pieces = sems.shape[1]
    depth = bx // pieces
    along = jnp.broadcast_to(factors[0:1, :], (by, nz))
    across = jnp.broadcast_to(factors[1:2, :], (by, nz))
    rows = pl.ds(PAD, by)
    copies = []
    for piece in range(pieces):
        def combine(i, _):
            x[i] = along * smooth[i, rows] - across * scaled[i, rows]
            r[i] = right[i] - along * image[i] + across * second[i]
            return 0

        lax.fori_loop(piece * depth, (piece + 1) * depth, combine, 0, unroll=2)
        part = pl.ds(piece * depth, depth)
        copies.append(pltpu.make_async_copy(x.at[part], x_hbm.at[0, part], sems.at[0, piece]))
        copies.append(pltpu.make_async_copy(r.at[part], r_hbm.at[0, part], sems.at[1, piece]))
        copies[-2].start()
        copies[-1].start()
    norms[0] = jnp.max(factors[2:3, :])
    norms[1] = jnp.max(factors[3:4, :])
    for copy in copies:
        copy.wait()


def body(right_side, cell_kind):
    n = lax.axis_size("gx")
    _, bx, by, nz = right_side.shape
    f32, i32 = jnp.float32, jnp.int32
    shape = (bx, by, nz)
    padded = (bx, by + 2 * PAD, nz)
    field = pltpu.VMEM(shape, f32)
    planes = pltpu.VMEM((2, by, nz), f32)
    edges = pltpu.VMEM((2, bx, 1, nz), f32)
    fields = pl.pallas_call(
        functools.partial(kernel, n),
        out_shape=tuple(
            jax.ShapeDtypeStruct(s, f32) for s in (shape, padded, shape, padded, shape, (8, nz))
        ),
        in_specs=[pl.BlockSpec(memory_space=pltpu.HBM)] * 2,
        out_specs=[pl.BlockSpec(memory_space=pltpu.VMEM)] * 6,
        scratch_shapes=[
            pltpu.VMEM(shape, i32), pltpu.VMEM(padded, f32),
            pltpu.VMEM((bx + 1, by, nz), f32), pltpu.VMEM((bx, by + PAD, nz), f32),
            field, field,
            pltpu.VMEM((2, by, nz), i32), planes, planes,
            pltpu.VMEM((2, bx, 1, nz), i32), pltpu.VMEM((2, bx, 1, nz), i32),
            edges, edges, edges, edges,
            pltpu.VMEM((n, 8, nz), f32),
            pltpu.SemaphoreType.DMA((2,)),
            pltpu.SemaphoreType.DMA((3, 4)),
            pltpu.SemaphoreType.DMA((3, 4)),
            pltpu.SemaphoreType.DMA,
            pltpu.SemaphoreType.DMA,
        ],
        compiler_params=pltpu.CompilerParams(
            collective_id=0, has_side_effects=True, vmem_limit_bytes=32 * 1024 * 1024
        ),
    )(cell_kind, right_side)
    x, r, norms = pl.pallas_call(
        finish,
        out_shape=(
            jax.ShapeDtypeStruct(right_side.shape, f32),
            jax.ShapeDtypeStruct(right_side.shape, f32),
            jax.ShapeDtypeStruct((2,), f32),
        ),
        in_specs=[pl.BlockSpec(memory_space=pltpu.VMEM)] * 6,
        out_specs=(
            pl.BlockSpec(memory_space=pltpu.HBM), pl.BlockSpec(memory_space=pltpu.HBM),
            pl.BlockSpec(memory_space=pltpu.SMEM),
        ),
        scratch_shapes=[field, field, pltpu.SemaphoreType.DMA((2, 4))],
        compiler_params=pltpu.CompilerParams(vmem_limit_bytes=16 * 1024 * 1024),
    )(*fields)
    return x, r, norms


def solution(mesh):
    spec = P(("member", "gx"), None, None, None)
    return jax.shard_map(
        body, mesh=mesh, in_specs=(spec, spec), out_specs=(spec, spec, P("member")),
        check_vma=False,
    )
```

```python
import functools

import jax
import jax.numpy as jnp
from jax import lax
from jax.experimental import pallas as pl
from jax.experimental.pallas import tpu as pltpu
from jax.sharding import PartitionSpec as P

GYB = 8
SHIFT_TERM = 0.1
PAD = 8
INNER_UNROLL = 4
STEP_UNROLL = 5
RIM_UNROLL = 5
MESH = pl.DeviceIdType.MESH


def inverse(value):
    guess = pl.reciprocal(value, approx=True)
    return guess * (2.0 - value * guess)


def conductivity_of(kind):
    power = jnp.left_shift(jnp.ones_like(kind), kind).astype(jnp.float32) * 0.25
    return jnp.where(kind > 0, power, 0.0)


def harmonic(first, second):
    return (2.0 * first) * second * inverse(jnp.maximum(first + second, 0.5))


def fold(value):
    return jnp.sum(value.reshape(-1, 8, value.shape[-1]), axis=0)


def kernel(
    n, kind_hbm, right_hbm, right, smooth, image, scaled, second, factors,
    kind, cond, face_x, face_y, face_z, inv,
    kind_x, right_x, smooth_x, scaled_x, kind_y, send_kind_y, right_y, send_right_y, cond_y,
    smooth_y, scaled_y, send_scaled_y, corner, send_corner, rim_x, rim_y,
    dots, in_sem, send_sem, recv_sem, dot_send, dot_recv,
):
    bx, by, nz = kind.shape
    rows = pl.ds(PAD, by)
    me = lax.axis_index("gx")
    column = lax.rem(me, GYB)
    line = lax.div(me, GYB)
    lines = n // GYB
    receives = [line > 0, line < lines - 1, column > 0, column < GYB - 1]
    sends = [line < lines - 1, line > 0, column < GYB - 1, column > 0]
    targets = [me + GYB, me - GYB, me + 1, me - 1]
    for low in (0, 1):
        for left in (2, 3):
            receives.append(jnp.logical_and(receives[low], receives[left]))
            sends.append(jnp.logical_and(sends[low], sends[left]))
            targets.append(targets[low] + targets[left] - me)

    barrier = pltpu.get_barrier_semaphore()

    def greet(k, _):
        pl.semaphore_signal(
            barrier, inc=1, device_id={"gx": lax.rem(me + k, n)}, device_id_type=MESH
        )
        return 0

    lax.fori_loop(1, n, greet, 0)

    load_kind = pltpu.make_async_copy(kind_hbm.at[0], kind, in_sem.at[0])
    load_right = pltpu.make_async_copy(right_hbm.at[0], right, in_sem.at[1])
    load_kind.start()
    load_right.start()

    copies = []

    def copy(side, src, dst):
        place = len(copies)
        copies.append((side, pltpu.make_async_remote_copy(
            src_ref=src, dst_ref=dst, send_sem=send_sem.at[place], recv_sem=recv_sem.at[place],
            device_id={"gx": targets[side]}, device_id_type=MESH,
        )))

    copy(0, kind_hbm.at[0, pl.ds(bx - 2, 2)], kind_x.at[0])
    copy(1, kind_hbm.at[0, pl.ds(0, 2)], kind_x.at[1])
    copy(2, send_kind_y.at[1], kind_y.at[0])
    copy(3, send_kind_y.at[0], kind_y.at[1])
    copy(0, right_hbm.at[0, bx - 1], right_x.at[0])
    copy(1, right_hbm.at[0, 0], right_x.at[1])
    copy(2, send_right_y.at[1], right_y.at[0])
    copy(3, send_right_y.at[0], right_y.at[1])
    for along_x in (0, 1):
        for along_y in (0, 1):
            copy(
                4 + 2 * along_x + along_y,
                send_corner.at[1 - along_x, 1 - along_y], corner.at[along_x, along_y],
            )
    copy(0, scaled.at[bx - 1, rows], scaled_x.at[0])
    copy(1, scaled.at[0, rows], scaled_x.at[1])
    copy(2, send_scaled_y.at[1], scaled_y.at[0])
    copy(3, send_scaled_y.at[0], scaled_y.at[1])

    def start(places):
        for place in places:
            side, item = copies[place]
            pl.when(sends[side])(item.start)

    def arrive(places):
        for place in places:
            side, item = copies[place]
            pl.when(receives[side])(item.wait_recv)

    for side in (0, 1):
        @pl.when(jnp.logical_not(receives[side]))
        def _():
            kind_x[side] = jnp.zeros((2, by, nz), jnp.int32)
            right_x[side] = jnp.zeros((by, nz), jnp.float32)
            scaled_x[side] = jnp.zeros((by, nz), jnp.float32)

        @pl.when(jnp.logical_not(receives[side + 2]))
        def _():
            kind_y[side] = jnp.zeros((2, bx, nz), jnp.int32)
            right_y[side] = jnp.zeros((bx, nz), jnp.float32)
            scaled_y[side] = jnp.zeros((bx, nz), jnp.float32)

        for other in (0, 1):
            @pl.when(jnp.logical_not(receives[4 + 2 * side + other]))
            def _():
                corner[side, other] = jnp.zeros((1, nz), jnp.int32)

    pl.semaphore_wait(barrier, n - 1)
    start((0, 1, 4, 5))
    load_kind.wait()

    def take_kind(i, _):
        one = pl.ds(i, 1)
        send_kind_y[0, 0, one, :] = kind[i, 0:1, :]
        send_kind_y[0, 1, one, :] = kind[i, 1:2, :]
        send_kind_y[1, 0, one, :] = kind[i, by - 1:by, :]
        send_kind_y[1, 1, one, :] = kind[i, by - 2:by - 1, :]
        return 0

    lax.fori_loop(0, bx, take_kind, 0, unroll=8)
    for side in (0, 1):
        for other in (0, 1):
            send_corner[side, other] = send_kind_y[other, 0, side * (bx - 1):side * (bx - 1) + 1, :]
    start((2, 3, 8, 9, 10, 11))
    load_right.wait()

    def take_right(i, _):
        send_right_y[0, pl.ds(i, 1), :] = right[i, 0:1, :]
        send_right_y[1, pl.ds(i, 1), :] = right[i, by - 1:by, :]
        return 0

    lax.fori_loop(0, bx, take_right, 0, unroll=8)
    start((6, 7))

    def conduct(i, _):
        cond[i, rows] = conductivity_of(kind[i])
        return 0

    lax.fori_loop(0, bx, conduct, 0, unroll=4)

    def faces_up(own):
        last_lane = lax.broadcasted_iota(jnp.int32, own.shape, 1) == nz - 1
        return harmonic(own, jnp.where(last_lane, 0.0, pltpu.roll(own, nz - 1, 1)))

    def face_along(i):
        own = cond[i, rows]
        face_z[i] = faces_up(own)
        return own

    def inner_faces(i, _):
        own = face_along(i)
        face_x[i] = harmonic(own, cond[i - 1, rows])
        return 0

    face_along(0)
    lax.fori_loop(1, bx, inner_faces, 0, unroll=INNER_UNROLL)

    def spread(buffer, field):
        def put(i, _):
            field[i, PAD - 1:PAD, :] = buffer[0, pl.ds(i, 1), :]
            field[i, PAD + by:PAD + by + 1, :] = buffer[1, pl.ds(i, 1), :]
            return 0

        lax.fori_loop(0, bx, put, 0, unroll=8)

    arrive((2, 3))
    for side in (0, 1):
        cond_y[side] = conductivity_of(kind_y[side, 0])
    spread(cond_y, cond)

    def prepare(i, sums):
        res_sq, gamma = sums
        own = cond[i, rows]
        face_y[i] = harmonic(
            cond[i, PAD:2 * PAD + by, :], cond[i, PAD - 1:2 * PAD + by - 1, :]
        )
        up = face_z[i]
        total = face_x[i] + face_x[i + 1]
        total = total + (face_y[i, 0:by, :] + face_y[i, 1:by + 1, :])
        total = total + (up + pltpu.roll(up, 1, 1))
        fluid = own > 0.0
        diagonal_inverse = inverse(jnp.where(fluid, SHIFT_TERM + total, 1.0))
        residual = jnp.where(fluid, right[i], 0.0)
        value = residual * diagonal_inverse
        right[i] = residual
        inv[i] = diagonal_inverse
        smooth[i, rows] = value
        return res_sq + fold(residual * residual), gamma + fold(residual * value)

    def neighbour_sum(field, i, first, count, below, above):
        own = field[i, pl.ds(PAD + first, count)]
        here = pl.ds(first, count)
        up = face_z[i, here]
        total = face_x[i, here] * below + face_x[i + 1, here] * above
        total = total + face_y[i, here] * field[i, pl.ds(PAD + first - 1, count)]
        total = total + face_y[i, pl.ds(first + 1, count)] * field[i, pl.ds(PAD + first + 1, count)]
        total = total + up * pltpu.roll(own, nz - 1, 1) + pltpu.roll(up * own, 1, 1)
        return own, total

    def apply(i, sums, first=0, count=by, below=None, above=None):
        delta, cross, square, mu = sums
        here, inside = pl.ds(first, count), pl.ds(PAD + first, count)
        below = smooth[i - 1, inside] if below is None else below
        above = smooth[i + 1, inside] if above is None else above
        own, total = neighbour_sum(smooth, i, first, count, below, above)
        residual = right[i, here]
        value = residual - total
        other = value * inv[i, here]
        image[i, here] = value
        scaled[i, inside] = other
        if first == 0:
            send_scaled_y[0, pl.ds(i, 1), :] = other[0:1, :]
        if first + count == by:
            send_scaled_y[1, pl.ds(i, 1), :] = other[count - 1:count, :]
        return (
            delta + fold(value * own), cross + fold(residual * value),
            square + fold(value * value), mu + fold(value * other),
        )

    def apply_again(i, nu, first=0, count=by, below=None, above=None):
        here, inside = pl.ds(first, count), pl.ds(PAD + first, count)
        below = scaled[i - 1, inside] if below is None else below
        above = scaled[i + 1, inside] if above is None else above
        own, total = neighbour_sum(scaled, i, first, count, below, above)
        value = image[i, here] - total
        second[i, here] = value
        return nu + fold(value * own)

    def halo(near, far, own, corners, source, rim):
        length = near.shape[0]
        rim[PAD:PAD + length, :] = near
        rim[PAD - 1:PAD, :] = conductivity_of(corners[0])
        rim[PAD + length:PAD + length + 1, :] = conductivity_of(corners[1])
        inner = harmonic(own, near)
        up = faces_up(near)
        total = inner + harmonic(near, far) + (up + pltpu.roll(up, 1, 1))
        total = total + harmonic(near, rim[PAD - 1:PAD - 1 + length, :])
        total = total + harmonic(near, rim[PAD + 1:PAD + 1 + length, :])
        fluid = near > 0.0
        value = jnp.where(fluid, source, 0.0) * inverse(jnp.where(fluid, SHIFT_TERM + total, 1.0))
        return inner, value

    def middle(step, sums):
        return lax.fori_loop(
            1, bx - 1, lambda i, s: step(i, s, PAD, by - 2 * PAD), sums, unroll=STEP_UNROLL
        )

    def rims(step, sums):
        def both(i, s):
            return step(i, step(i, s, 0, PAD), by - PAD, PAD)

        return lax.fori_loop(1, bx - 1, both, sums, unroll=RIM_UNROLL)

    def ends(step, sums, field, halo):
        sums = step(0, sums, below=halo[0])
        return step(bx - 1, sums, above=halo[1])

    zero = jnp.zeros((8, nz), jnp.float32)
    sums = lax.fori_loop(1, bx - 1, prepare, (zero, zero), unroll=STEP_UNROLL)
    arrive((8, 9, 10, 11, 6, 7))
    for side in (0, 1):
        _, smooth_y[side] = halo(
            cond_y[side], conductivity_of(kind_y[side, 1]), conductivity_of(send_kind_y[side, 0]),
            (corner[0, side], corner[1, side]), right_y[side], rim_y,
        )
    spread(smooth_y, smooth)
    arrive((0, 1, 4, 5))
    for side in (0, 1):
        face_x[side * bx], smooth_x[side] = halo(
            conductivity_of(kind_x[side, 1 - side]), conductivity_of(kind_x[side, side]),
            cond[side * (bx - 1), rows], (corner[side, 0], corner[side, 1]), right_x[side], rim_x,
        )
    res_sq, gamma = prepare(bx - 1, prepare(0, sums))
    sums = ends(apply, (zero,) * 4, smooth, smooth_x)
    start((12, 13))
    delta, cross, square, mu = lax.fori_loop(1, bx - 1, apply, sums, unroll=STEP_UNROLL)
    start((14, 15))
    nu = middle(apply_again, zero)
    arrive((14, 15))
    spread(scaled_y, scaled)
    nu = rims(apply_again, nu)
    arrive((12, 13))
    nu = ends(apply_again, nu, scaled, scaled_x)

    parts = (res_sq, gamma, delta, cross, square, mu, nu)
    row = lax.broadcasted_iota(jnp.int32, (8, nz), 0)
    message = zero
    for place, part in enumerate(parts):
        message = jnp.where(row == place, jnp.sum(part, axis=0, keepdims=True), message)
    dots[me] = message

    def tell(k, _):
        pltpu.make_async_remote_copy(
            src_ref=dots.at[me], dst_ref=dots.at[me], send_sem=dot_send, recv_sem=dot_recv,
            device_id={"gx": lax.rem(me + k, n)}, device_id_type=MESH,
        ).start()
        return 0

    lax.fori_loop(1, n, tell, 0)
    most = dots.at[pl.ds(0, n - 1)]
    for side, item in copies:
        pl.when(sends[side])(item.wait_send)
    pltpu.make_async_copy(most, most, dot_recv).wait()

    total = jnp.sum(jnp.sum(dots[...], axis=0), axis=1, keepdims=True)
    res_sq, gamma, delta, cross, square, mu, nu = (total[k:k + 1, :] for k in range(7))
    alpha = gamma / delta
    gamma_next = gamma - 2.0 * alpha * delta + alpha * alpha * mu
    delta_next = delta - 2.0 * alpha * mu + alpha * alpha * nu
    res_sq_next = res_sq - 2.0 * alpha * cross + alpha * alpha * square
    beta = gamma_next / gamma
    alpha_next = gamma_next / (delta_next - beta * gamma_next / alpha)
    along = alpha + alpha_next * (1.0 + beta)
    across = alpha * alpha_next
    cells = n * bx * by * nz
    result = jnp.where(row == 0, along, across)
    result = jnp.where(row == 2, res_sq / cells, result)
    factors[...] = jnp.where(row == 3, res_sq_next / cells, result)
    pltpu.make_async_copy(most, most, dot_send).wait()


def finish(right, smooth, image, scaled, second, factors, x_hbm, r_hbm, norms, x, r, sems):
    bx, by, nz = right.shape
    pieces = sems.shape[1]
    depth = bx // pieces
    along = jnp.broadcast_to(factors[0:1, :], (by, nz))
    across = jnp.broadcast_to(factors[1:2, :], (by, nz))
    rows = pl.ds(PAD, by)
    copies = []
    for piece in range(pieces):
        def combine(i, _):
            x[i] = along * smooth[i, rows] - across * scaled[i, rows]
            r[i] = right[i] - along * image[i] + across * second[i]
            return 0

        lax.fori_loop(piece * depth, (piece + 1) * depth, combine, 0, unroll=2)
        part = pl.ds(piece * depth, depth)
        copies.append(pltpu.make_async_copy(x.at[part], x_hbm.at[0, part], sems.at[0, piece]))
        copies.append(pltpu.make_async_copy(r.at[part], r_hbm.at[0, part], sems.at[1, piece]))
        copies[-2].start()
        copies[-1].start()
    norms[0] = jnp.max(factors[2:3, :])
    norms[1] = jnp.max(factors[3:4, :])
    for copy in copies:
        copy.wait()


def body(right_side, cell_kind):
    n = lax.axis_size("gx")
    _, bx, by, nz = right_side.shape
    f32, i32 = jnp.float32, jnp.int32
    shape = (bx, by, nz)
    padded = (bx, by + 2 * PAD, nz)
    field = pltpu.VMEM(shape, f32)
    planes = pltpu.VMEM((2, by, nz), f32)
    edges = pltpu.VMEM((2, bx, nz), f32)
    fields = pl.pallas_call(
        functools.partial(kernel, n),
        out_shape=tuple(
            jax.ShapeDtypeStruct(s, f32) for s in (shape, padded, shape, padded, shape, (8, nz))
        ),
        in_specs=[pl.BlockSpec(memory_space=pltpu.HBM)] * 2,
        out_specs=[pl.BlockSpec(memory_space=pltpu.VMEM)] * 6,
        scratch_shapes=[
            pltpu.VMEM(shape, i32), pltpu.VMEM(padded, f32),
            pltpu.VMEM((bx + 1, by, nz), f32), pltpu.VMEM((bx, by + PAD, nz), f32),
            field, field,
            pltpu.VMEM((2, 2, by, nz), i32), planes, planes, planes,
            pltpu.VMEM((2, 2, bx, nz), i32), pltpu.VMEM((2, 2, bx, nz), i32),
            edges, edges, edges, edges, edges, edges,
            pltpu.VMEM((2, 2, 1, nz), i32), pltpu.VMEM((2, 2, 1, nz), i32),
            pltpu.VMEM((by + 2 * PAD, nz), f32), pltpu.VMEM((bx + 2 * PAD, nz), f32),
            pltpu.VMEM((n, 8, nz), f32),
            pltpu.SemaphoreType.DMA((2,)),
            pltpu.SemaphoreType.DMA((16,)),
            pltpu.SemaphoreType.DMA((16,)),
            pltpu.SemaphoreType.DMA,
            pltpu.SemaphoreType.DMA,
        ],
        compiler_params=pltpu.CompilerParams(
            collective_id=0, has_side_effects=True, vmem_limit_bytes=32 * 1024 * 1024
        ),
    )(
        pltpu.with_memory_space_constraint(cell_kind, pltpu.HBM),
        pltpu.with_memory_space_constraint(right_side, pltpu.HBM),
    )
    x, r, norms = pl.pallas_call(
        finish,
        out_shape=(
            jax.ShapeDtypeStruct(right_side.shape, f32),
            jax.ShapeDtypeStruct(right_side.shape, f32),
            jax.ShapeDtypeStruct((2,), f32),
        ),
        in_specs=[pl.BlockSpec(memory_space=pltpu.VMEM)] * 6,
        out_specs=(
            pl.BlockSpec(memory_space=pltpu.HBM), pl.BlockSpec(memory_space=pltpu.HBM),
            pl.BlockSpec(memory_space=pltpu.SMEM),
        ),
        scratch_shapes=[field, field, pltpu.SemaphoreType.DMA((2, 4))],
        compiler_params=pltpu.CompilerParams(vmem_limit_bytes=16 * 1024 * 1024),
    )(*fields)
    return x, r, norms


def solution(mesh):
    spec = P(("member", "gx"), None, None, None)
    return jax.shard_map(
        body, mesh=mesh, in_specs=(spec, spec), out_specs=(spec, spec, P("member")),
        check_vma=False,
    )
```

```python
import functools

import jax
import jax.numpy as jnp
from jax import lax
from jax.experimental import pallas as pl
from jax.experimental.pallas import tpu as pltpu
from jax.sharding import PartitionSpec as P

GYB = 8
SHIFT_TERM = 0.1
PAD = 8
INNER_UNROLL = 4
STEP_UNROLL = 5
RIM_UNROLL = 5
MESH = pl.DeviceIdType.MESH


def inverse(value):
    guess = pl.reciprocal(value, approx=True)
    return guess * (2.0 - value * guess)


def conductivity_of(kind):
    power = jnp.left_shift(jnp.ones_like(kind), kind).astype(jnp.float32) * 0.25
    return jnp.where(kind > 0, power, 0.0)


def harmonic(first, second):
    return (2.0 * first) * second * inverse(jnp.maximum(first + second, 0.5))


def fold(value):
    return jnp.sum(value.reshape(-1, 8, value.shape[-1]), axis=0)


def kernel(
    n, kind_hbm, right_hbm, right, smooth, image, scaled, second, factors,
    kind, cond, face_x, face_y, face_z, inv,
    kind_x, right_x, smooth_x, scaled_x, kind_y, send_kind_y, right_y, send_right_y, cond_y,
    smooth_y, scaled_y, send_scaled_y, corner, send_corner, rim_x, rim_y,
    dots, in_sem, send_sem, recv_sem, dot_send, dot_recv,
):
    bx, by, nz = kind.shape
    rows = pl.ds(PAD, by)
    me = lax.axis_index("gx")
    column = lax.rem(me, GYB)
    line = lax.div(me, GYB)
    lines = n // GYB
    receives = [line > 0, line < lines - 1, column > 0, column < GYB - 1]
    sends = [line < lines - 1, line > 0, column < GYB - 1, column > 0]
    targets = [me + GYB, me - GYB, me + 1, me - 1]
    for low in (0, 1):
        for left in (2, 3):
            receives.append(jnp.logical_and(receives[low], receives[left]))
            sends.append(jnp.logical_and(sends[low], sends[left]))
            targets.append(targets[low] + targets[left] - me)

    load_kind = pltpu.make_async_copy(kind_hbm.at[0], kind, in_sem.at[0])
    load_right = pltpu.make_async_copy(right_hbm.at[0], right, in_sem.at[1])
    load_kind.start()
    load_right.start()
    barrier = pltpu.get_barrier_semaphore()

    def greet(k, _):
        pl.semaphore_signal(
            barrier, inc=1, device_id={"gx": lax.rem(me + k, n)}, device_id_type=MESH
        )
        return 0

    lax.fori_loop(1, n, greet, 0, unroll=15)


    copies = []

    def copy(side, src, dst):
        place = len(copies)
        copies.append((side, pltpu.make_async_remote_copy(
            src_ref=src, dst_ref=dst, send_sem=send_sem.at[place], recv_sem=recv_sem.at[place],
            device_id={"gx": targets[side]}, device_id_type=MESH,
        )))

    copy(0, kind.at[pl.ds(bx - 2, 2)], kind_x.at[0])
    copy(1, kind.at[pl.ds(0, 2)], kind_x.at[1])
    copy(2, send_kind_y.at[1], kind_y.at[0])
    copy(3, send_kind_y.at[0], kind_y.at[1])
    copy(0, right_hbm.at[0, bx - 1], right_x.at[0])
    copy(1, right_hbm.at[0, 0], right_x.at[1])
    copy(2, send_right_y.at[1], right_y.at[0])
    copy(3, send_right_y.at[0], right_y.at[1])
    for along_x in (0, 1):
        for along_y in (0, 1):
            copy(
                4 + 2 * along_x + along_y,
                send_corner.at[1 - along_x, 1 - along_y], corner.at[along_x, along_y],
            )
    copy(0, scaled.at[bx - 1, rows], scaled_x.at[0])
    copy(1, scaled.at[0, rows], scaled_x.at[1])
    copy(2, send_scaled_y.at[1], scaled_y.at[0])
    copy(3, send_scaled_y.at[0], scaled_y.at[1])

    def start(places):
        for place in places:
            side, item = copies[place]
            pl.when(sends[side])(item.start)

    def arrive(places):
        for place in places:
            side, item = copies[place]
            pl.when(receives[side])(item.wait_recv)

    for side in (0, 1):
        @pl.when(jnp.logical_not(receives[side]))
        def _():
            kind_x[side] = jnp.zeros((2, by, nz), jnp.int32)
            right_x[side] = jnp.zeros((by, nz), jnp.float32)
            scaled_x[side] = jnp.zeros((by, nz), jnp.float32)

        @pl.when(jnp.logical_not(receives[side + 2]))
        def _():
            kind_y[side] = jnp.zeros((2, bx, nz), jnp.int32)
            right_y[side] = jnp.zeros((bx, nz), jnp.float32)
            scaled_y[side] = jnp.zeros((bx, nz), jnp.float32)

        for other in (0, 1):
            @pl.when(jnp.logical_not(receives[4 + 2 * side + other]))
            def _():
                corner[side, other] = jnp.zeros((1, nz), jnp.int32)

    pl.semaphore_wait(barrier, n - 1)
    load_kind.wait()
    start((0, 1, 4, 5))

    def take_kind(i, _):
        one = pl.ds(i, 1)
        send_kind_y[0, 0, one, :] = kind[i, 0:1, :]
        send_kind_y[0, 1, one, :] = kind[i, 1:2, :]
        send_kind_y[1, 0, one, :] = kind[i, by - 1:by, :]
        send_kind_y[1, 1, one, :] = kind[i, by - 2:by - 1, :]
        return 0

    lax.fori_loop(0, bx, take_kind, 0, unroll=8)
    for side in (0, 1):
        for other in (0, 1):
            send_corner[side, other] = send_kind_y[other, 0, side * (bx - 1):side * (bx - 1) + 1, :]
    start((2, 3, 8, 9, 10, 11))
    load_right.wait()

    def take_right(i, _):
        send_right_y[0, pl.ds(i, 1), :] = right[i, 0:1, :]
        send_right_y[1, pl.ds(i, 1), :] = right[i, by - 1:by, :]
        return 0

    lax.fori_loop(0, bx, take_right, 0, unroll=8)
    start((6, 7))

    def conduct(i, _):
        cond[i, rows] = conductivity_of(kind[i])
        return 0

    lax.fori_loop(0, bx, conduct, 0, unroll=4)

    def faces_up(own):
        last_lane = lax.broadcasted_iota(jnp.int32, own.shape, 1) == nz - 1
        return harmonic(own, jnp.where(last_lane, 0.0, pltpu.roll(own, nz - 1, 1)))

    def face_along(i):
        own = cond[i, rows]
        face_z[i] = faces_up(own)
        return own

    def inner_faces(i, _):
        own = face_along(i)
        face_x[i] = harmonic(own, cond[i - 1, rows])
        return 0

    face_along(0)
    lax.fori_loop(1, bx, inner_faces, 0, unroll=INNER_UNROLL)

    def spread(buffer, field):
        def put(i, _):
            field[i, PAD - 1:PAD, :] = buffer[0, pl.ds(i, 1), :]
            field[i, PAD + by:PAD + by + 1, :] = buffer[1, pl.ds(i, 1), :]
            return 0

        lax.fori_loop(0, bx, put, 0, unroll=8)

    arrive((2, 3))
    for side in (0, 1):
        cond_y[side] = conductivity_of(kind_y[side, 0])
    spread(cond_y, cond)

    def prepare(i, sums):
        res_sq, gamma = sums
        own = cond[i, rows]
        face_y[i] = harmonic(
            cond[i, PAD:2 * PAD + by, :], cond[i, PAD - 1:2 * PAD + by - 1, :]
        )
        up = face_z[i]
        total = face_x[i] + face_x[i + 1]
        total = total + (face_y[i, 0:by, :] + face_y[i, 1:by + 1, :])
        total = total + (up + pltpu.roll(up, 1, 1))
        fluid = own > 0.0
        diagonal_inverse = inverse(jnp.where(fluid, SHIFT_TERM + total, 1.0))
        residual = jnp.where(fluid, right[i], 0.0)
        value = residual * diagonal_inverse
        right[i] = residual
        inv[i] = diagonal_inverse
        smooth[i, rows] = value
        return res_sq + fold(residual * residual), gamma + fold(residual * value)

    def neighbour_sum(field, i, first, count, below, above):
        own = field[i, pl.ds(PAD + first, count)]
        here = pl.ds(first, count)
        up = face_z[i, here]
        total = face_x[i, here] * below + face_x[i + 1, here] * above
        total = total + face_y[i, here] * field[i, pl.ds(PAD + first - 1, count)]
        total = total + face_y[i, pl.ds(first + 1, count)] * field[i, pl.ds(PAD + first + 1, count)]
        total = total + up * pltpu.roll(own, nz - 1, 1) + pltpu.roll(up * own, 1, 1)
        return own, total

    def apply(i, sums, first=0, count=by, below=None, above=None):
        delta, cross, square, mu = sums
        here, inside = pl.ds(first, count), pl.ds(PAD + first, count)
        below = smooth[i - 1, inside] if below is None else below
        above = smooth[i + 1, inside] if above is None else above
        own, total = neighbour_sum(smooth, i, first, count, below, above)
        residual = right[i, here]
        value = residual - total
        other = value * inv[i, here]
        image[i, here] = value
        scaled[i, inside] = other
        if first == 0:
            send_scaled_y[0, pl.ds(i, 1), :] = other[0:1, :]
        if first + count == by:
            send_scaled_y[1, pl.ds(i, 1), :] = other[count - 1:count, :]
        return (
            delta + fold(value * own), cross + fold(residual * value),
            square + fold(value * value), mu + fold(value * other),
        )

    def apply_again(i, nu, first=0, count=by, below=None, above=None):
        here, inside = pl.ds(first, count), pl.ds(PAD + first, count)
        below = scaled[i - 1, inside] if below is None else below
        above = scaled[i + 1, inside] if above is None else above
        own, total = neighbour_sum(scaled, i, first, count, below, above)
        value = image[i, here] - total
        second[i, here] = value
        return nu + fold(value * own)

    def halo(near, far, own, corners, source, rim):
        length = near.shape[0]
        rim[PAD:PAD + length, :] = near
        rim[PAD - 1:PAD, :] = conductivity_of(corners[0])
        rim[PAD + length:PAD + length + 1, :] = conductivity_of(corners[1])
        inner = harmonic(own, near)
        up = faces_up(near)
        total = inner + harmonic(near, far) + (up + pltpu.roll(up, 1, 1))
        total = total + harmonic(near, rim[PAD - 1:PAD - 1 + length, :])
        total = total + harmonic(near, rim[PAD + 1:PAD + 1 + length, :])
        fluid = near > 0.0
        value = jnp.where(fluid, source, 0.0) * inverse(jnp.where(fluid, SHIFT_TERM + total, 1.0))
        return inner, value

    def middle(step, sums):
        return lax.fori_loop(
            1, bx - 1, lambda i, s: step(i, s, PAD, by - 2 * PAD), sums, unroll=STEP_UNROLL
        )

    def rims(step, sums):
        def both(i, s):
            return step(i, step(i, s, 0, PAD), by - PAD, PAD)

        return lax.fori_loop(1, bx - 1, both, sums, unroll=RIM_UNROLL)

    def ends(step, sums, field, halo):
        sums = step(0, sums, below=halo[0])
        return step(bx - 1, sums, above=halo[1])

    zero = jnp.zeros((8, nz), jnp.float32)
    sums = lax.fori_loop(1, bx - 1, prepare, (zero, zero), unroll=STEP_UNROLL)
    arrive((8, 9, 10, 11, 6, 7))
    for side in (0, 1):
        _, smooth_y[side] = halo(
            cond_y[side], conductivity_of(kind_y[side, 1]), conductivity_of(send_kind_y[side, 0]),
            (corner[0, side], corner[1, side]), right_y[side], rim_y,
        )
    spread(smooth_y, smooth)
    arrive((0, 1, 4, 5))
    for side in (0, 1):
        face_x[side * bx], smooth_x[side] = halo(
            conductivity_of(kind_x[side, 1 - side]), conductivity_of(kind_x[side, side]),
            cond[side * (bx - 1), rows], (corner[side, 0], corner[side, 1]), right_x[side], rim_x,
        )
    res_sq, gamma = prepare(bx - 1, prepare(0, sums))
    sums = ends(apply, (zero,) * 4, smooth, smooth_x)
    start((12, 13))
    delta, cross, square, mu = lax.fori_loop(1, bx - 1, apply, sums, unroll=STEP_UNROLL)
    start((14, 15))
    nu = middle(apply_again, zero)
    arrive((14, 15))
    spread(scaled_y, scaled)
    nu = rims(apply_again, nu)
    arrive((12, 13))
    nu = ends(apply_again, nu, scaled, scaled_x)

    parts = (res_sq, gamma, delta, cross, square, mu, nu)
    row = lax.broadcasted_iota(jnp.int32, (8, nz), 0)
    message = zero
    for place, part in enumerate(parts):
        message = jnp.where(row == place, jnp.sum(part, axis=0, keepdims=True), message)
    dots[me] = message

    def tell(k, _):
        pltpu.make_async_remote_copy(
            src_ref=dots.at[me], dst_ref=dots.at[me], send_sem=dot_send, recv_sem=dot_recv,
            device_id={"gx": lax.rem(me + k, n)}, device_id_type=MESH,
        ).start()
        return 0

    lax.fori_loop(1, n, tell, 0)
    most = dots.at[pl.ds(0, n - 1)]
    for side, item in copies:
        pl.when(sends[side])(item.wait_send)
    pltpu.make_async_copy(most, most, dot_recv).wait()

    total = jnp.sum(jnp.sum(dots[...], axis=0), axis=1, keepdims=True)
    res_sq, gamma, delta, cross, square, mu, nu = (total[k:k + 1, :] for k in range(7))
    alpha = gamma / delta
    gamma_next = gamma - 2.0 * alpha * delta + alpha * alpha * mu
    delta_next = delta - 2.0 * alpha * mu + alpha * alpha * nu
    res_sq_next = res_sq - 2.0 * alpha * cross + alpha * alpha * square
    beta = gamma_next / gamma
    alpha_next = gamma_next / (delta_next - beta * gamma_next / alpha)
    along = alpha + alpha_next * (1.0 + beta)
    across = alpha * alpha_next
    cells = n * bx * by * nz
    result = jnp.where(row == 0, along, across)
    result = jnp.where(row == 2, res_sq / cells, result)
    factors[...] = jnp.where(row == 3, res_sq_next / cells, result)
    pltpu.make_async_copy(most, most, dot_send).wait()


def finish(right, smooth, image, scaled, second, factors, x_hbm, r_hbm, norms, x, r, sems):
    bx, by, nz = right.shape
    pieces = sems.shape[1]
    depth = bx // pieces
    along = jnp.broadcast_to(factors[0:1, :], (by, nz))
    across = jnp.broadcast_to(factors[1:2, :], (by, nz))
    rows = pl.ds(PAD, by)
    copies = []
    for piece in range(pieces):
        def combine(i, _):
            x[i] = along * smooth[i, rows] - across * scaled[i, rows]
            r[i] = right[i] - along * image[i] + across * second[i]
            return 0

        lax.fori_loop(piece * depth, (piece + 1) * depth, combine, 0, unroll=8)
        part = pl.ds(piece * depth, depth)
        copies.append(pltpu.make_async_copy(x.at[part], x_hbm.at[0, part], sems.at[0, piece]))
        copies.append(pltpu.make_async_copy(r.at[part], r_hbm.at[0, part], sems.at[1, piece]))
        copies[-2].start()
        copies[-1].start()
    norms[0] = jnp.max(factors[2:3, :])
    norms[1] = jnp.max(factors[3:4, :])
    for copy in copies:
        copy.wait()


def body(right_side, cell_kind):
    n = lax.axis_size("gx")
    _, bx, by, nz = right_side.shape
    f32, i32 = jnp.float32, jnp.int32
    shape = (bx, by, nz)
    padded = (bx, by + 2 * PAD, nz)
    field = pltpu.VMEM(shape, f32)
    planes = pltpu.VMEM((2, by, nz), f32)
    edges = pltpu.VMEM((2, bx, nz), f32)
    fields = pl.pallas_call(
        functools.partial(kernel, n),
        out_shape=tuple(
            jax.ShapeDtypeStruct(s, f32) for s in (shape, padded, shape, padded, shape, (8, nz))
        ),
        in_specs=[pl.BlockSpec(memory_space=pltpu.HBM)] * 2,
        out_specs=[pl.BlockSpec(memory_space=pltpu.VMEM)] * 6,
        scratch_shapes=[
            pltpu.VMEM(shape, i32), pltpu.VMEM(padded, f32),
            pltpu.VMEM((bx + 1, by, nz), f32), pltpu.VMEM((bx, by + PAD, nz), f32),
            field, field,
            pltpu.VMEM((2, 2, by, nz), i32), planes, planes, planes,
            pltpu.VMEM((2, 2, bx, nz), i32), pltpu.VMEM((2, 2, bx, nz), i32),
            edges, edges, edges, edges, edges, edges,
            pltpu.VMEM((2, 2, 1, nz), i32), pltpu.VMEM((2, 2, 1, nz), i32),
            pltpu.VMEM((by + 2 * PAD, nz), f32), pltpu.VMEM((bx + 2 * PAD, nz), f32),
            pltpu.VMEM((n, 8, nz), f32),
            pltpu.SemaphoreType.DMA((2,)),
            pltpu.SemaphoreType.DMA((16,)),
            pltpu.SemaphoreType.DMA((16,)),
            pltpu.SemaphoreType.DMA,
            pltpu.SemaphoreType.DMA,
        ],
        compiler_params=pltpu.CompilerParams(
            collective_id=0, has_side_effects=True, vmem_limit_bytes=32 * 1024 * 1024
        ),
    )(
        pltpu.with_memory_space_constraint(cell_kind, pltpu.HBM),
        pltpu.with_memory_space_constraint(right_side, pltpu.HBM),
    )
    x, r, norms = pl.pallas_call(
        finish,
        out_shape=(
            jax.ShapeDtypeStruct(right_side.shape, f32),
            jax.ShapeDtypeStruct(right_side.shape, f32),
            jax.ShapeDtypeStruct((2,), f32),
        ),
        in_specs=[pl.BlockSpec(memory_space=pltpu.VMEM)] * 6,
        out_specs=(
            pl.BlockSpec(memory_space=pltpu.HBM), pl.BlockSpec(memory_space=pltpu.HBM),
            pl.BlockSpec(memory_space=pltpu.SMEM),
        ),
        scratch_shapes=[field, field, pltpu.SemaphoreType.DMA((2, 4))],
        compiler_params=pltpu.CompilerParams(vmem_limit_bytes=16 * 1024 * 1024),
    )(*fields)
    return x, r, norms


def solution(mesh):
    spec = P(("member", "gx"), None, None, None)
    return jax.shard_map(
        body, mesh=mesh, in_specs=(spec, spec), out_specs=(spec, spec, P("member")),
        check_vma=False,
    )
```

```python
import functools

import jax
import jax.numpy as jnp
from jax import lax
from jax.experimental import pallas as pl
from jax.experimental.pallas import tpu as pltpu
from jax.sharding import PartitionSpec as P

GYB = 8
SHIFT_TERM = 0.1
PAD = 8
INNER_UNROLL = 4
STEP_UNROLL = 5
RIM_UNROLL = 5
MESH = pl.DeviceIdType.MESH


def inverse(value):
    guess = pl.reciprocal(value, approx=True)
    return guess * (2.0 - value * guess)


def conductivity_of(kind):
    power = jnp.left_shift(jnp.ones_like(kind), kind).astype(jnp.float32) * 0.25
    return jnp.where(kind > 0, power, 0.0)


def harmonic(first, second):
    return (2.0 * first) * second * inverse(jnp.maximum(first + second, 0.5))


def fold(value):
    return jnp.sum(value.reshape(-1, 8, value.shape[-1]), axis=0)


def kernel(
    n, kind_hbm, right_hbm, right, smooth, image, scaled, second, factors,
    kind, cond, face_x, face_y, face_z, inv,
    kind_x, right_x, smooth_x, scaled_x, kind_y, send_kind_y, right_y, send_right_y, cond_y,
    smooth_y, scaled_y, send_scaled_y, corner, send_corner, rim_x, rim_y,
    dots, in_sem, send_sem, recv_sem, dot_send, dot_recv,
):
    bx, by, nz = kind.shape
    rows = pl.ds(PAD, by)
    me = lax.axis_index("gx")
    column = lax.rem(me, GYB)
    line = lax.div(me, GYB)
    lines = n // GYB
    receives = [line > 0, line < lines - 1, column > 0, column < GYB - 1]
    sends = [line < lines - 1, line > 0, column < GYB - 1, column > 0]
    targets = [me + GYB, me - GYB, me + 1, me - 1]
    for low in (0, 1):
        for left in (2, 3):
            receives.append(jnp.logical_and(receives[low], receives[left]))
            sends.append(jnp.logical_and(sends[low], sends[left]))
            targets.append(targets[low] + targets[left] - me)

    load_kind = pltpu.make_async_copy(kind_hbm.at[0], kind, in_sem.at[0])
    load_right = pltpu.make_async_copy(right_hbm.at[0], right, in_sem.at[1])
    load_kind.start()
    load_right.start()
    barrier = pltpu.get_barrier_semaphore()

    def greet(k, _):
        pl.semaphore_signal(
            barrier, inc=1, device_id={"gx": lax.rem(me + k, n)}, device_id_type=MESH
        )
        return 0

    lax.fori_loop(1, n, greet, 0, unroll=15)


    copies = []

    def copy(side, src, dst):
        place = len(copies)
        copies.append((side, pltpu.make_async_remote_copy(
            src_ref=src, dst_ref=dst, send_sem=send_sem.at[place], recv_sem=recv_sem.at[place],
            device_id={"gx": targets[side]}, device_id_type=MESH,
        )))

    copy(0, kind.at[pl.ds(bx - 2, 2)], kind_x.at[0])
    copy(1, kind.at[pl.ds(0, 2)], kind_x.at[1])
    copy(2, send_kind_y.at[1], kind_y.at[0])
    copy(3, send_kind_y.at[0], kind_y.at[1])
    copy(0, right_hbm.at[0, bx - 1], right_x.at[0])
    copy(1, right_hbm.at[0, 0], right_x.at[1])
    copy(2, send_right_y.at[1], right_y.at[0])
    copy(3, send_right_y.at[0], right_y.at[1])
    for along_x in (0, 1):
        for along_y in (0, 1):
            copy(
                4 + 2 * along_x + along_y,
                send_corner.at[1 - along_x, 1 - along_y], corner.at[along_x, along_y],
            )
    copy(0, scaled.at[bx - 1, rows], scaled_x.at[0])
    copy(1, scaled.at[0, rows], scaled_x.at[1])
    copy(2, send_scaled_y.at[1], scaled_y.at[0])
    copy(3, send_scaled_y.at[0], scaled_y.at[1])

    def start(places):
        for place in places:
            side, item = copies[place]
            pl.when(sends[side])(item.start)

    def arrive(places):
        for place in places:
            side, item = copies[place]
            pl.when(receives[side])(item.wait_recv)

    for side in (0, 1):
        @pl.when(jnp.logical_not(receives[side]))
        def _():
            kind_x[side] = jnp.zeros((2, by, nz), jnp.int32)
            right_x[side] = jnp.zeros((by, nz), jnp.float32)
            scaled_x[side] = jnp.zeros((by, nz), jnp.float32)

        @pl.when(jnp.logical_not(receives[side + 2]))
        def _():
            kind_y[side] = jnp.zeros((2, bx, nz), jnp.int32)
            right_y[side] = jnp.zeros((bx, nz), jnp.float32)
            scaled_y[side] = jnp.zeros((bx, nz), jnp.float32)

        for other in (0, 1):
            @pl.when(jnp.logical_not(receives[4 + 2 * side + other]))
            def _():
                corner[side, other] = jnp.zeros((1, nz), jnp.int32)

    load_kind.wait()
    def take_kind(i, _):
        one = pl.ds(i, 1)
        send_kind_y[0, 0, one, :] = kind[i, 0:1, :]
        send_kind_y[0, 1, one, :] = kind[i, 1:2, :]
        send_kind_y[1, 0, one, :] = kind[i, by - 1:by, :]
        send_kind_y[1, 1, one, :] = kind[i, by - 2:by - 1, :]
        return 0

    lax.fori_loop(0, bx, take_kind, 0, unroll=8)
    for side in (0, 1):
        for other in (0, 1):
            send_corner[side, other] = send_kind_y[other, 0, side * (bx - 1):side * (bx - 1) + 1, :]
    load_right.wait()

    def take_right(i, _):
        send_right_y[0, pl.ds(i, 1), :] = right[i, 0:1, :]
        send_right_y[1, pl.ds(i, 1), :] = right[i, by - 1:by, :]
        return 0

    lax.fori_loop(0, bx, take_right, 0, unroll=8)
    pl.semaphore_wait(barrier, n - 1)
    start((0, 1, 2, 3, 8, 9, 10, 11, 4, 5, 6, 7))

    def conduct(i, _):
        cond[i, rows] = conductivity_of(kind[i])
        return 0

    lax.fori_loop(0, bx, conduct, 0, unroll=4)

    def faces_up(own):
        last_lane = lax.broadcasted_iota(jnp.int32, own.shape, 1) == nz - 1
        return harmonic(own, jnp.where(last_lane, 0.0, pltpu.roll(own, nz - 1, 1)))

    def face_along(i):
        own = cond[i, rows]
        face_z[i] = faces_up(own)
        return own

    def inner_faces(i, _):
        own = face_along(i)
        face_x[i] = harmonic(own, cond[i - 1, rows])
        return 0

    face_along(0)
    lax.fori_loop(1, bx, inner_faces, 0, unroll=INNER_UNROLL)

    def spread(buffer, field):
        def put(i, _):
            field[i, PAD - 1:PAD, :] = buffer[0, pl.ds(i, 1), :]
            field[i, PAD + by:PAD + by + 1, :] = buffer[1, pl.ds(i, 1), :]
            return 0

        lax.fori_loop(0, bx, put, 0, unroll=8)

    arrive((2, 3))
    for side in (0, 1):
        cond_y[side] = conductivity_of(kind_y[side, 0])
    spread(cond_y, cond)

    def prepare(i, sums):
        res_sq, gamma = sums
        own = cond[i, rows]
        face_y[i] = harmonic(
            cond[i, PAD:2 * PAD + by, :], cond[i, PAD - 1:2 * PAD + by - 1, :]
        )
        up = face_z[i]
        total = face_x[i] + face_x[i + 1]
        total = total + (face_y[i, 0:by, :] + face_y[i, 1:by + 1, :])
        total = total + (up + pltpu.roll(up, 1, 1))
        fluid = own > 0.0
        diagonal_inverse = inverse(jnp.where(fluid, SHIFT_TERM + total, 1.0))
        residual = jnp.where(fluid, right[i], 0.0)
        value = residual * diagonal_inverse
        right[i] = residual
        inv[i] = diagonal_inverse
        smooth[i, rows] = value
        return res_sq + fold(residual * residual), gamma + fold(residual * value)

    def neighbour_sum(field, i, first, count, below, above):
        own = field[i, pl.ds(PAD + first, count)]
        here = pl.ds(first, count)
        up = face_z[i, here]
        total = face_x[i, here] * below + face_x[i + 1, here] * above
        total = total + face_y[i, here] * field[i, pl.ds(PAD + first - 1, count)]
        total = total + face_y[i, pl.ds(first + 1, count)] * field[i, pl.ds(PAD + first + 1, count)]
        total = total + up * pltpu.roll(own, nz - 1, 1) + pltpu.roll(up * own, 1, 1)
        return own, total

    def apply(i, sums, first=0, count=by, below=None, above=None):
        delta, cross, square, mu = sums
        here, inside = pl.ds(first, count), pl.ds(PAD + first, count)
        below = smooth[i - 1, inside] if below is None else below
        above = smooth[i + 1, inside] if above is None else above
        own, total = neighbour_sum(smooth, i, first, count, below, above)
        residual = right[i, here]
        value = residual - total
        other = value * inv[i, here]
        image[i, here] = value
        scaled[i, inside] = other
        if first == 0:
            send_scaled_y[0, pl.ds(i, 1), :] = other[0:1, :]
        if first + count == by:
            send_scaled_y[1, pl.ds(i, 1), :] = other[count - 1:count, :]
        return (
            delta + fold(value * own), cross + fold(residual * value),
            square + fold(value * value), mu + fold(value * other),
        )

    def apply_again(i, nu, first=0, count=by, below=None, above=None):
        here, inside = pl.ds(first, count), pl.ds(PAD + first, count)
        below = scaled[i - 1, inside] if below is None else below
        above = scaled[i + 1, inside] if above is None else above
        own, total = neighbour_sum(scaled, i, first, count, below, above)
        value = image[i, here] - total
        second[i, here] = value
        return nu + fold(value * own)

    def halo(near, far, own, corners, source, rim):
        length = near.shape[0]
        rim[PAD:PAD + length, :] = near
        rim[PAD - 1:PAD, :] = conductivity_of(corners[0])
        rim[PAD + length:PAD + length + 1, :] = conductivity_of(corners[1])
        inner = harmonic(own, near)
        up = faces_up(near)
        total = inner + harmonic(near, far) + (up + pltpu.roll(up, 1, 1))
        total = total + harmonic(near, rim[PAD - 1:PAD - 1 + length, :])
        total = total + harmonic(near, rim[PAD + 1:PAD + 1 + length, :])
        fluid = near > 0.0
        value = jnp.where(fluid, source, 0.0) * inverse(jnp.where(fluid, SHIFT_TERM + total, 1.0))
        return inner, value

    def middle(step, sums):
        return lax.fori_loop(
            1, bx - 1, lambda i, s: step(i, s, PAD, by - 2 * PAD), sums, unroll=STEP_UNROLL
        )

    def rims(step, sums):
        def both(i, s):
            return step(i, step(i, s, 0, PAD), by - PAD, PAD)

        return lax.fori_loop(1, bx - 1, both, sums, unroll=RIM_UNROLL)

    def ends(step, sums, field, halo):
        sums = step(0, sums, below=halo[0])
        return step(bx - 1, sums, above=halo[1])

    zero = jnp.zeros((8, nz), jnp.float32)
    sums = lax.fori_loop(1, bx - 1, prepare, (zero, zero), unroll=STEP_UNROLL)
    arrive((8, 9, 10, 11, 6, 7))
    for side in (0, 1):
        _, smooth_y[side] = halo(
            cond_y[side], conductivity_of(kind_y[side, 1]), conductivity_of(send_kind_y[side, 0]),
            (corner[0, side], corner[1, side]), right_y[side], rim_y,
        )
    spread(smooth_y, smooth)
    arrive((0, 1, 4, 5))
    for side in (0, 1):
        face_x[side * bx], smooth_x[side] = halo(
            conductivity_of(kind_x[side, 1 - side]), conductivity_of(kind_x[side, side]),
            cond[side * (bx - 1), rows], (corner[side, 0], corner[side, 1]), right_x[side], rim_x,
        )
    res_sq, gamma = prepare(bx - 1, prepare(0, sums))
    sums = ends(apply, (zero,) * 4, smooth, smooth_x)
    start((12, 13))
    delta, cross, square, mu = lax.fori_loop(1, bx - 1, apply, sums, unroll=STEP_UNROLL)
    start((14, 15))
    nu = middle(apply_again, zero)
    arrive((14, 15))
    spread(scaled_y, scaled)
    nu = rims(apply_again, nu)
    arrive((12, 13))
    nu = ends(apply_again, nu, scaled, scaled_x)

    parts = (res_sq, gamma, delta, cross, square, mu, nu)
    row = lax.broadcasted_iota(jnp.int32, (8, nz), 0)
    message = zero
    for place, part in enumerate(parts):
        message = jnp.where(row == place, jnp.sum(part, axis=0, keepdims=True), message)
    dots[me] = message

    def tell(k, _):
        pltpu.make_async_remote_copy(
            src_ref=dots.at[me], dst_ref=dots.at[me], send_sem=dot_send, recv_sem=dot_recv,
            device_id={"gx": lax.rem(me + k, n)}, device_id_type=MESH,
        ).start()
        return 0

    lax.fori_loop(1, n, tell, 0)
    most = dots.at[pl.ds(0, n - 1)]
    for side, item in copies:
        pl.when(sends[side])(item.wait_send)
    pltpu.make_async_copy(most, most, dot_recv).wait()

    total = jnp.sum(jnp.sum(dots[...], axis=0), axis=1, keepdims=True)
    res_sq, gamma, delta, cross, square, mu, nu = (total[k:k + 1, :] for k in range(7))
    alpha = gamma / delta
    gamma_next = gamma - 2.0 * alpha * delta + alpha * alpha * mu
    delta_next = delta - 2.0 * alpha * mu + alpha * alpha * nu
    res_sq_next = res_sq - 2.0 * alpha * cross + alpha * alpha * square
    beta = gamma_next / gamma
    alpha_next = gamma_next / (delta_next - beta * gamma_next / alpha)
    along = alpha + alpha_next * (1.0 + beta)
    across = alpha * alpha_next
    cells = n * bx * by * nz
    result = jnp.where(row == 0, along, across)
    result = jnp.where(row == 2, res_sq / cells, result)
    factors[...] = jnp.where(row == 3, res_sq_next / cells, result)
    pltpu.make_async_copy(most, most, dot_send).wait()


def finish(right, smooth, image, scaled, second, factors, x_hbm, r_hbm, norms, x, r, sems):
    bx, by, nz = right.shape
    pieces = sems.shape[1]
    depth = bx // pieces
    along = jnp.broadcast_to(factors[0:1, :], (by, nz))
    across = jnp.broadcast_to(factors[1:2, :], (by, nz))
    rows = pl.ds(PAD, by)
    copies = []
    for piece in range(pieces):
        def combine(i, _):
            x[i] = along * smooth[i, rows] - across * scaled[i, rows]
            r[i] = right[i] - along * image[i] + across * second[i]
            return 0

        lax.fori_loop(piece * depth, (piece + 1) * depth, combine, 0, unroll=8)
        part = pl.ds(piece * depth, depth)
        copies.append(pltpu.make_async_copy(x.at[part], x_hbm.at[0, part], sems.at[0, piece]))
        copies.append(pltpu.make_async_copy(r.at[part], r_hbm.at[0, part], sems.at[1, piece]))
        copies[-2].start()
        copies[-1].start()
    norms[0] = jnp.max(factors[2:3, :])
    norms[1] = jnp.max(factors[3:4, :])
    for copy in copies:
        copy.wait()


def body(right_side, cell_kind):
    n = lax.axis_size("gx")
    _, bx, by, nz = right_side.shape
    f32, i32 = jnp.float32, jnp.int32
    shape = (bx, by, nz)
    padded = (bx, by + 2 * PAD, nz)
    field = pltpu.VMEM(shape, f32)
    planes = pltpu.VMEM((2, by, nz), f32)
    edges = pltpu.VMEM((2, bx, nz), f32)
    fields = pl.pallas_call(
        functools.partial(kernel, n),
        out_shape=tuple(
            jax.ShapeDtypeStruct(s, f32) for s in (shape, padded, shape, padded, shape, (8, nz))
        ),
        in_specs=[pl.BlockSpec(memory_space=pltpu.HBM)] * 2,
        out_specs=[pl.BlockSpec(memory_space=pltpu.VMEM)] * 6,
        scratch_shapes=[
            pltpu.VMEM(shape, i32), pltpu.VMEM(padded, f32),
            pltpu.VMEM((bx + 1, by, nz), f32), pltpu.VMEM((bx, by + PAD, nz), f32),
            field, field,
            pltpu.VMEM((2, 2, by, nz), i32), planes, planes, planes,
            pltpu.VMEM((2, 2, bx, nz), i32), pltpu.VMEM((2, 2, bx, nz), i32),
            edges, edges, edges, edges, edges, edges,
            pltpu.VMEM((2, 2, 1, nz), i32), pltpu.VMEM((2, 2, 1, nz), i32),
            pltpu.VMEM((by + 2 * PAD, nz), f32), pltpu.VMEM((bx + 2 * PAD, nz), f32),
            pltpu.VMEM((n, 8, nz), f32),
            pltpu.SemaphoreType.DMA((2,)),
            pltpu.SemaphoreType.DMA((16,)),
            pltpu.SemaphoreType.DMA((16,)),
            pltpu.SemaphoreType.DMA,
            pltpu.SemaphoreType.DMA,
        ],
        compiler_params=pltpu.CompilerParams(
            collective_id=0, has_side_effects=True, vmem_limit_bytes=32 * 1024 * 1024
        ),
    )(
        pltpu.with_memory_space_constraint(cell_kind, pltpu.HBM),
        pltpu.with_memory_space_constraint(right_side, pltpu.HBM),
    )
    x, r, norms = pl.pallas_call(
        finish,
        out_shape=(
            jax.ShapeDtypeStruct(right_side.shape, f32),
            jax.ShapeDtypeStruct(right_side.shape, f32),
            jax.ShapeDtypeStruct((2,), f32),
        ),
        in_specs=[pl.BlockSpec(memory_space=pltpu.VMEM)] * 6,
        out_specs=(
            pl.BlockSpec(memory_space=pltpu.HBM), pl.BlockSpec(memory_space=pltpu.HBM),
            pl.BlockSpec(memory_space=pltpu.SMEM),
        ),
        scratch_shapes=[field, field, pltpu.SemaphoreType.DMA((2, 4))],
        compiler_params=pltpu.CompilerParams(vmem_limit_bytes=16 * 1024 * 1024),
    )(*fields)
    return x, r, norms


def solution(mesh):
    spec = P(("member", "gx"), None, None, None)
    return jax.shard_map(
        body, mesh=mesh, in_specs=(spec, spec), out_specs=(spec, spec, P("member")),
        check_vma=False,
    )
```
